256 devices in a mesh: gx: 32 (over y, z), gy: 2 (over x_lo), gz: 4 (over x_hi, core).
Axes of the slice: x: 4 (x_hi: 2, x_lo: 2; x = x_hi * 2 + x_lo), y: 4, z: 8, core: 2. Of those that a mesh axis runs over, the one named last changes fastest.
Arguments:
- tokens: bfloat16 [640, 14336], P(('gx', 'gy'), 'gz'), may hold values from -6 to 6
- first_weight: bfloat16 [14336, 28672], P('gz', ('gx', 'gy')), may hold values from -0.046875 to 0.046875
- first_bias: bfloat16 [1, 28672], P(None, ('gx', 'gy')), may hold values from -3 to 3
- second_weight: bfloat16 [28672, 14336], P(('gx', 'gy'), 'gz'), may hold values from -0.03125 to 0.03125
- second_bias: bfloat16 [14336], P('gz'), may hold values from -3 to 3
- out_grad: bfloat16 [640, 14336], P(('gx', 'gy'), 'gz'), may hold values from -1.1953125 to 1.1953125
Outputs:
- output: bfloat16 [640, 14336], P(('gx', 'gy'), 'gz')
- tokens_grad: bfloat16 [640, 14336], P(('gx', 'gy'), 'gz')
- first_weight_grad: bfloat16 [14336, 28672], P('gz', ('gx', 'gy'))
- first_bias_grad: bfloat16 [1, 28672], P(None, ('gx', 'gy'))
- second_weight_grad: bfloat16 [28672, 14336], P(('gx', 'gy'), 'gz')
- second_bias_grad: bfloat16 [14336], P('gz')
The draws below stay inside these ranges and needn't reach their ends.
All inputs are finite; a program needn't handle non-finite values.
Results may differ from the reference program's by a relative error of at most 0.022.
Values may be sent and summed in bfloat16 or wider, within the bound.
No kernel may reach another device: no remote copies, remote signals or barrier semaphores. Data moves between devices by JAX's collectives and lax.ppermute only.
A program may use at most 128 MiB of HBM per device.

```python
import jax
import jax.numpy as jnp
from jax import lax

D = 14336
FF = 28672
TOKENS = 640
N_GX = 32
N_GY = 2


def steps_of(stream_key, shape, pieces, low, largest):
    gain = 1.0
    for axis_at, blocks in pieces:
        heights = jax.random.uniform(jax.random.fold_in(jax.random.fold_in(stream_key, 6), axis_at), (blocks,), jnp.float32, low / len(pieces), largest / len(pieces))
        gain = gain * jnp.repeat(jnp.exp(heights), shape[axis_at] // blocks).reshape((-1,) + (1,) * (len(shape) - 1 - axis_at))
    return gain


def normal_values(rng, dims, deviation, most, shards=(), dtype=jnp.bfloat16):
    factor_of = steps_of(rng, dims, shards, -0.22, 0.18) if shards else 1.0
    values = jax.random.normal(rng, dims, jnp.float32) * deviation * factor_of
    return jnp.minimum(jnp.maximum(values, -most), most).astype(dtype)


def setup_inputs(seed: int = 0) -> dict:
    seeds = jax.random.split(jax.random.key(seed), 7)
    return {
        "tokens": normal_values(seeds[0], (TOKENS, D), 1.0, 6.0, ((0, 64), (1, 4))),
        "first_weight": normal_values(seeds[1], (D, FF), D ** -0.5, 0.046875, ((0, 4), (1, 64))),
        "first_bias": normal_values(seeds[2], (1, FF), 0.5, 3.0, ((1, 64),)),
        "second_weight": normal_values(seeds[3], (FF, D), FF ** -0.5, 0.03125, ((0, 64), (1, 4))),
        "second_bias": normal_values(seeds[4], (D,), 0.5, 3.0, ((0, 4),)),
        "out_grad": normal_values(seeds[5], (TOKENS, D), 0.2, 1.1953125, ((0, 64), (1, 4))),
    }


gelu_scale = 0.7978845608028654
gelu_cubic = 0.044715


def gelu_parts(pre_act):
    inner = gelu_scale * (pre_act + gelu_cubic * pre_act * pre_act * pre_act)
    tangent = jnp.tanh(inner)
    gelu_val = 0.5 * pre_act * (1.0 + tangent)
    derivative = 0.5 * (1.0 + tangent) + 0.5 * pre_act * (1.0 - tangent * tangent) * gelu_scale * (1.0 + 3.0 * gelu_cubic * pre_act * pre_act)
    return gelu_val, derivative


def group_rows(array, member):
    columns = array.shape[-1]
    return array.reshape(N_GX, N_GY, -1, columns)[:, member].reshape(-1, columns)


def rounded(value):
    return lax.optimization_barrier(value.astype(jnp.bfloat16)).astype(jnp.float32)


def reference(tokens, first_weight, first_bias, second_weight, second_bias, out_grad):
    pre_act = jnp.dot(tokens, first_weight, preferred_element_type=jnp.float32) + first_bias.astype(jnp.float32)
    gelu_val, derivative = gelu_parts(pre_act)
    hidden = gelu_val.astype(jnp.bfloat16)
    output = (jnp.dot(hidden, second_weight, preferred_element_type=jnp.float32) + second_bias.astype(jnp.float32)).astype(jnp.bfloat16)
    grad_hidden = jnp.dot(out_grad, second_weight.T, preferred_element_type=jnp.float32)
    grad_pre = (grad_hidden * derivative).astype(jnp.bfloat16)
    tokens_grad = jnp.dot(grad_pre, first_weight.T, preferred_element_type=jnp.float32).astype(jnp.bfloat16)
    weight_first = jnp.zeros((D, FF), jnp.float32)
    bias_first = jnp.zeros((1, FF), jnp.float32)
    weight_second = jnp.zeros((FF, D), jnp.float32)
    for member in range(N_GY):
        token_part = group_rows(tokens, member)
        pre_part = group_rows(grad_pre, member)
        hidden_part = group_rows(hidden, member)
        grad_part = group_rows(out_grad, member)
        weight_first = weight_first + rounded(jnp.dot(token_part.T, pre_part, preferred_element_type=jnp.float32))
        bias_first = bias_first + rounded(jnp.sum(pre_part.astype(jnp.float32), axis=0, keepdims=True))
        weight_second = weight_second + rounded(jnp.dot(hidden_part.T, grad_part, preferred_element_type=jnp.float32))
    second_bias_grad = jnp.sum(out_grad.astype(jnp.float32), axis=0).astype(jnp.bfloat16)
    return (output, tokens_grad, weight_first.astype(jnp.bfloat16), bias_first.astype(jnp.bfloat16), weight_second.astype(jnp.bfloat16), second_bias_grad)
```

```python
import jax
import jax.numpy as jnp
import numpy as np
from jax import lax
from jax.experimental import pallas as pl
from jax.experimental.pallas import tpu as pltpu
from jax.sharding import PartitionSpec as P

N_Y, N_Z = 4, 8
CHUNK = 7
gelu_scale = 0.7978845608028654
gelu_cubic = 0.044715
f32, bf16 = jnp.float32, jnp.bfloat16


def gelu_parts(pre_act):
    inner = gelu_scale * (pre_act + gelu_cubic * pre_act * pre_act * pre_act)
    tangent = jnp.tanh(inner)
    gelu_val = 0.5 * pre_act * (1.0 + tangent)
    derivative = 0.5 * (1.0 + tangent) + 0.5 * pre_act * (1.0 - tangent * tangent) * gelu_scale * (
        1.0 + 3.0 * gelu_cubic * pre_act * pre_act
    )
    return (gelu_val, derivative)


def contract_rows(left, right):
    return lax.dot_general(left, right, (((0,), (0,)), ((), ())), preferred_element_type=f32)


def contract_cols(left, right):
    return lax.dot_general(left, right, (((1,), (1,)), ((), ())), preferred_element_type=f32)


def along_y(value, hops):
    pairs = [
        (y * N_Z + z, (y + hops) % N_Y * N_Z + z) for y in range(N_Y) for z in range(N_Z)
    ]
    return lax.ppermute(value, "gx", pairs)


def along_z(value, hops):
    pairs = [
        (y * N_Z + z, y * N_Z + (z + hops) % N_Z) for y in range(N_Y) for z in range(N_Z)
    ]
    return lax.ppermute(value, "gx", pairs)


def swap_x_lo(value):
    return lax.ppermute(value, "gy", [(0, 1), (1, 0)])


def swap_x_hi(value):
    return lax.ppermute(value, "gz", [(i, i ^ 2) for i in range(4)])


def swap_core(value):
    return lax.ppermute(value, "gz", [(i, i ^ 1) for i in range(4)])


def rows_of(*blocks):
    return jnp.concatenate(blocks, axis=0)


def add(left, right):
    return (left.astype(f32) + right.astype(f32)).astype(bf16)


def gather_z(own):
    half = own.shape[1] // 2
    up, down = [own], [own]
    for _ in range(3):
        up.append(along_z(up[-1], 1))
        down.append(along_z(down[-1], -1))
    far = along_z(up[3][:, :half], 1), along_z(down[3][:, half:], -1)
    return [own, down[1], up[1], down[2], up[2], down[3], up[3]], far


def gather_z_small(own):
    up, down = [own], [own]
    for _ in range(3):
        up.append(along_z(up[-1], 1))
        down.append(along_z(down[-1], -1))
    return join(own, down[1], up[1], down[2], up[2], down[3], up[3], along_z(up[3], 1))


def gather_y_small(own):
    return join(own, along_y(own, -1), along_y(own, 1), along_y(own, 2))


def gather_y(own):
    half = own.shape[1] // 2
    low, high = along_y(own, 1), along_y(own, -1)
    far = along_y(low[:, :half], 1), along_y(high[:, half:], -1)
    return [own, high, low], far


def scatter_z(terms):
    own, p1, m1, p2, m2, p3, m3, far = terms
    half = own.shape[1] // 2
    up = along_z(far[:, :half], 1)
    down = along_z(far[:, half:], -1)
    up = jnp.concatenate([add(up, p3[:, :half]), p3[:, half:]], axis=1)
    down = jnp.concatenate([m3[:, :half], add(down, m3[:, half:])], axis=1)
    up, down = along_z(up, 1), along_z(down, -1)
    up, down = along_z(add(up, p2), 1), along_z(add(down, m2), -1)
    up, down = along_z(add(up, p1), 1), along_z(add(down, m1), -1)
    return own, up, down


def scatter_z_small(terms):
    own, p1, m1, p2, m2, p3, m3, far = terms
    up = along_z(add(along_z(far, 1), p3), 1)
    down = along_z(m3, -1)
    up, down = along_z(add(up, p2), 1), along_z(add(down, m2), -1)
    up, down = along_z(add(up, p1), 1), along_z(add(down, m1), -1)
    return own.astype(f32) + up.astype(f32) + down.astype(f32)


def scatter_y_small(terms):
    own, p1, m1, far = terms
    moved = along_y(p1, 1), along_y(m1, -1), along_y(far, 2)
    return sum([m.astype(f32) for m in moved], own.astype(f32))


def scatter_y(terms):
    own, p1, m1, far = terms
    half = own.shape[1] // 2
    up = along_y(far[:, :half], 1)
    down = along_y(far[:, half:], -1)
    up_b = along_y(p1[:, half:], 1)
    down_b = along_y(m1[:, :half], -1)
    up_a = along_y(add(up, p1[:, :half]), 1)
    down_a = along_y(add(down, m1[:, half:]), -1)
    up = jnp.concatenate([up_a, up_b], axis=1)
    down = jnp.concatenate([down_b, down_a], axis=1)
    return own, up, down


def turn_matrix(rows, first, second):
    source = np.arange(rows).reshape(first, second, -1).transpose(1, 0, 2).reshape(-1)
    return jnp.asarray(np.eye(rows, dtype=np.float32)[source], bf16)


def params():
    return pltpu.CompilerParams(vmem_limit_bytes=40 * 2**20)


def cost(flops, moved):
    return pl.CostEstimate(flops=int(flops), bytes_accessed=int(moved), transcendentals=0)


def gather_matmul(blocks, far, weight, transposed, core, turn):
    n_blocks = len(blocks)
    size, width = blocks[0].shape
    rows = size * (n_blocks + (1 if far else 0))
    hidden = weight.shape[0] if transposed else weight.shape[1]
    steps = 4
    chunk = width // steps
    half = rows // 2
    n_far = len(far)

    def kernel(*refs):
        core_ref, *refs = refs
        block_refs, refs = refs[:n_blocks], refs[n_blocks:]
        far_refs, refs = refs[:n_far], refs[n_far:]
        weight_ref, *refs = refs
        turn_ref = refs.pop(0) if turn is not None else None
        all_ref, keep_ref, give_ref, total, turned = refs
        step = pl.program_id(0)
        for i, ref in enumerate(block_refs):
            all_ref[i * size : (i + 1) * size, :] = ref[...]
        if far:
            at = n_blocks * size

            @pl.when(step < steps // 2)
            def _():
                all_ref[at:, :] = far_refs[0][...]

            @pl.when(step >= steps // 2)
            def _():
                all_ref[at:, :] = far_refs[1][...]

        dims = ((1,), (1,)) if transposed else ((1,), (0,))
        term = lax.dot_general(
            all_ref[...], weight_ref[...], (dims, ((), ())), preferred_element_type=f32
        )

        @pl.when(step == 0)
        def _():
            total[...] = term

        @pl.when(step > 0)
        def _():
            total[...] += term

        @pl.when(step == steps - 1)
        def _():
            result = total[...]
            if turn_ref is not None:
                result = jnp.dot(
                    turn_ref[...], result.astype(bf16), preferred_element_type=f32
                )
            turned[...] = result
            mine = core_ref[0]
            keep_ref[...] = turned[pl.ds(pl.multiple_of(mine * half, half), half), :]
            give_ref[...] = turned[pl.ds(pl.multiple_of((1 - mine) * half, half), half), :].astype(bf16)

    in_specs = [pl.BlockSpec(memory_space=pltpu.SMEM)]
    in_specs += [pl.BlockSpec((size, chunk), lambda i: (0, i)) for _ in blocks]
    if far:
        in_specs += [
            pl.BlockSpec((size, chunk), lambda i: (0, jnp.minimum(i, steps // 2 - 1))),
            pl.BlockSpec((size, chunk), lambda i: (0, jnp.maximum(i - steps // 2, 0))),
        ]
    in_specs.append(
        pl.BlockSpec((hidden, chunk), lambda i: (0, i))
        if transposed
        else pl.BlockSpec((chunk, hidden), lambda i: (i, 0))
    )
    extra = []
    if turn is not None:
        extra = [turn]
        in_specs.append(pl.BlockSpec((rows, rows), lambda i: (0, 0)))
    fixed = pl.BlockSpec((half, hidden), lambda i: (0, 0))
    return pl.pallas_call(
        kernel,
        grid=(steps,),
        in_specs=in_specs,
        out_specs=[pl.BlockSpec((rows, chunk), lambda i: (0, i)), fixed, fixed],
        out_shape=[
            jax.ShapeDtypeStruct((rows, width), bf16),
            jax.ShapeDtypeStruct((half, hidden), f32),
            jax.ShapeDtypeStruct((half, hidden), bf16),
        ],
        scratch_shapes=[pltpu.VMEM((rows, hidden), f32), pltpu.VMEM((rows, hidden), f32)],
        compiler_params=params(),
        cost_estimate=cost(2 * rows * width * hidden, 2 * (2 * rows * width + width * hidden)),
    )(core, *blocks, *far, weight, *extra)


def matmul_scatter(own, other, weight, transposed, core, turn, turn_terms, n_blocks):
    half, hidden = own.shape
    rows = 2 * half
    width = weight.shape[0] if transposed else weight.shape[1]
    steps = CHUNK
    chunk = width // steps
    size = rows // n_blocks

    def kernel(core_ref, own_ref, other_ref, weight_ref, turn_ref, full_ref, turned_ref, *outs):
        @pl.when(pl.program_id(0) == 0)
        def _():
            mine = core_ref[0]
            full_ref[pl.ds(pl.multiple_of(mine * half, half), half), :] = own_ref[...]
            full_ref[pl.ds(pl.multiple_of((1 - mine) * half, half), half), :] = other_ref[...]
            turned_ref[...] = jnp.dot(
                turn_ref[...], full_ref[...], preferred_element_type=f32
            ).astype(bf16)

        dims = ((1,), (1,)) if transposed else ((1,), (0,))
        left = turned_ref if turn_terms else full_ref
        term = lax.dot_general(
            left[...], weight_ref[...], (dims, ((), ())), preferred_element_type=f32
        ).astype(bf16)
        for i, out in enumerate(outs):
            out[...] = term[i * size : (i + 1) * size]

    fixed = pl.BlockSpec((rows, hidden), lambda i: (0, 0))
    part = pl.BlockSpec((half, hidden), lambda i: (0, 0))
    return pl.pallas_call(
        kernel,
        grid=(steps,),
        in_specs=[
            pl.BlockSpec(memory_space=pltpu.SMEM),
            part,
            part,
            pl.BlockSpec((chunk, hidden), lambda i: (i, 0))
            if transposed
            else pl.BlockSpec((hidden, chunk), lambda i: (0, i)),
            pl.BlockSpec((rows, rows), lambda i: (0, 0)),
        ],
        out_specs=[fixed, fixed] + [pl.BlockSpec((size, chunk), lambda i: (0, i))] * n_blocks,
        out_shape=[jax.ShapeDtypeStruct((rows, hidden), bf16)] * 2
        + [jax.ShapeDtypeStruct((size, width), bf16)] * n_blocks,
        compiler_params=params(),
        cost_estimate=cost(2 * rows * width * hidden, 2 * (rows * width + width * hidden)),
    )(core, own, other, weight, turn)


def join(*blocks):
    width = blocks[0].shape[1]
    rows = sum(b.shape[0] for b in blocks)
    chunk = width // CHUNK

    def kernel(*refs):
        *ins, out = refs
        out[...] = jnp.concatenate([r[...].astype(f32) for r in ins], axis=0).astype(bf16)

    return pl.pallas_call(
        kernel,
        grid=(CHUNK,),
        in_specs=[pl.BlockSpec((b.shape[0], chunk), lambda i: (0, i)) for b in blocks],
        out_specs=pl.BlockSpec((rows, chunk), lambda i: (0, i)),
        out_shape=jax.ShapeDtypeStruct((rows, width), bf16),
        compiler_params=params(),
        cost_estimate=cost(rows * width, 4 * rows * width),
    )(*blocks)


def sum_split(n_blocks, *terms):
    rows, width = terms[0].shape
    chunk = width // CHUNK
    size = rows // n_blocks

    def kernel(*refs):
        ins, outs = refs[: len(terms)], refs[len(terms) :]
        total = ins[0][...].astype(f32)
        for r in ins[1:]:
            total += r[...].astype(f32)
        for i, out in enumerate(outs):
            out[...] = total[i * size : (i + 1) * size].astype(bf16)

    return pl.pallas_call(
        kernel,
        grid=(CHUNK,),
        in_specs=[pl.BlockSpec((rows, chunk), lambda i: (0, i)) for _ in terms],
        out_specs=[pl.BlockSpec((size, chunk), lambda i: (0, i))] * n_blocks,
        out_shape=[jax.ShapeDtypeStruct((size, width), bf16)] * n_blocks,
        compiler_params=params(),
        cost_estimate=cost(rows * width, 2 * (len(terms) + 1) * rows * width),
    )(*terms)


def half_sum(keep, give):
    chip = (keep + swap_core(give).astype(f32)).astype(bf16)
    return chip.astype(f32) + swap_x_hi(chip).astype(f32)


def column_sums(blocks):
    def ring_z(rows):
        r = [rows[20 * i : 20 * (i + 1)].astype(f32) for i in range(N_Z)]
        zero, p1, m1, p2, m2, p3, m3, far = r
        return ((zero + far) + (p2 + m2)) + ((p1 + m3) + (m1 + p3))

    own, p1, m1, far = [ring_z(blocks[160 * i : 160 * (i + 1)]) for i in range(N_Y)]
    total = (own + far) + (p1 + m1)
    total = total[:10] + total[10:]
    return jnp.sum(total, axis=0)


def shards(tokens, first_weight, first_bias, second_weight, second_bias, out_grad):
    core = lax.axis_index("gz").astype(jnp.int32).reshape(1) % 2
    rows = 640
    to_y, to_z = turn_matrix(rows, N_Z, N_Y), turn_matrix(rows, N_Y, N_Z)
    other = swap_x_lo(rows_of(tokens, out_grad))
    tokens_x, grad_x = rows_of(tokens, other[:10]), rows_of(out_grad, other[10:])

    token_rows, keep, give = gather_matmul(
        *gather_z(gather_y_small(tokens_x)), first_weight, False, core, to_y
    )
    pre_act = half_sum(keep, give) + first_bias.astype(f32)
    gelu_val, derivative = gelu_parts(pre_act)
    hidden_half = gelu_val.astype(bf16)
    hidden, _, *out_terms = matmul_scatter(
        hidden_half, swap_core(hidden_half), second_weight, False, core, to_z, True, N_Z
    )

    grad_rows, keep, give = gather_matmul(
        *gather_y(gather_z_small(grad_x)), second_weight, True, core, None
    )
    grad_half = (half_sum(keep, give) * derivative).astype(bf16)
    grad_pre, grad_pre_z, *in_terms = matmul_scatter(
        grad_half, swap_core(grad_half), first_weight, True, core, to_z, False, N_Y
    )

    out_rows = scatter_y_small(sum_split(N_Y, *scatter_z(out_terms))).astype(bf16)
    output = (
        out_rows[:10].astype(f32) + swap_x_lo(out_rows[10:]).astype(f32) + second_bias.astype(f32)
    ).astype(bf16)

    in_rows = scatter_z_small(sum_split(N_Z, *scatter_y(in_terms))).astype(bf16)
    tokens_grad = add(in_rows[:10], swap_x_lo(in_rows[10:]))

    first_grad = contract_rows(token_rows, grad_pre_z).astype(bf16)
    bias_grad = jnp.sum(grad_pre.astype(f32), axis=0, keepdims=True).astype(bf16)
    second_grad = contract_rows(hidden, grad_rows).astype(bf16)
    return (
        output,
        tokens_grad,
        first_grad,
        bias_grad,
        second_grad,
        column_sums(grad_rows).astype(bf16),
    )


def solution(mesh):
    placed = (
        P(("gx", "gy"), "gz"),
        P("gz", ("gx", "gy")),
        P(None, ("gx", "gy")),
        P(("gx", "gy"), "gz"),
        P("gz"),
        P(("gx", "gy"), "gz"),
    )
    return jax.shard_map(
        shards,
        mesh=mesh,
        in_specs=placed,
        out_specs=(
            P(("gx", "gy"), "gz"),
            P(("gx", "gy"), "gz"),
            P("gz", ("gx", "gy")),
            P(None, ("gx", "gy")),
            P(("gx", "gy"), "gz"),
            P("gz"),
        ),
        check_vma=False,
    )
```

```python
import jax
import jax.numpy as jnp
import numpy as np
from jax import lax
from jax.experimental import pallas as pl
from jax.experimental.pallas import tpu as pltpu
from jax.sharding import PartitionSpec as P

N_Y, N_Z = 4, 8
CHUNKS = 7
LIMIT = 16
gelu_scale = 0.7978845608028654
gelu_cubic = 0.044715
f32, bf16 = jnp.float32, jnp.bfloat16


def gelu_parts(pre_act):
    inner = gelu_scale * (pre_act + gelu_cubic * pre_act * pre_act * pre_act)
    tangent = jnp.tanh(inner)
    gelu_val = 0.5 * pre_act * (1.0 + tangent)
    derivative = 0.5 * (1.0 + tangent) + 0.5 * pre_act * (1.0 - tangent * tangent) * gelu_scale * (
        1.0 + 3.0 * gelu_cubic * pre_act * pre_act
    )
    return (gelu_val, derivative)


def contract_rows(left, right):
    return lax.dot_general(left, right, (((0,), (0,)), ((), ())), preferred_element_type=f32)


def contract_cols(left, right):
    return lax.dot_general(left, right, (((1,), (1,)), ((), ())), preferred_element_type=f32)


def along_y(value, hops):
    pairs = [
        (y * N_Z + z, (y + hops) % N_Y * N_Z + z) for y in range(N_Y) for z in range(N_Z)
    ]
    return lax.ppermute(value, "gx", pairs)


def along_z(value, hops):
    pairs = [
        (y * N_Z + z, y * N_Z + (z + hops) % N_Z) for y in range(N_Y) for z in range(N_Z)
    ]
    return lax.ppermute(value, "gx", pairs)


def swap_x_lo(value):
    return lax.ppermute(value, "gy", [(0, 1), (1, 0)])


def swap_x_hi(value):
    return lax.ppermute(value, "gz", [(i, i ^ 2) for i in range(4)])


def swap_core(value):
    return lax.ppermute(value, "gz", [(i, i ^ 1) for i in range(4)])


def rows_of(*blocks):
    return jnp.concatenate(blocks, axis=0)


def tie(*values):
    return lax.optimization_barrier(values)


def add(left, right):
    return (left.astype(f32) + right.astype(f32)).astype(bf16)


def gather_both(tokens_x, grad_x):
    g_up1, g_down1 = along_z(grad_x, 1), along_z(grad_x, -1)
    small = [along_y(tokens_x, -1), along_y(tokens_x, 1), along_y(tokens_x, 2)]
    g_up2, g_down2 = along_z(g_up1, 1), along_z(g_down1, -1)
    own = join(tokens_x, *small)
    cut = own.shape[1] // CHUNKS * (CHUNKS // 2)
    g_up3, g_down3 = along_z(g_up2, 1), along_z(g_down2, -1)
    own, g_up3, g_down3 = tie(own, g_up3, g_down3)
    up1, down1 = along_z(own, 1), along_z(own, -1)
    g_own = join(grad_x, g_down1, g_up1, g_down2, g_up2, g_down3, g_up3, along_z(g_up3, 1))
    up1, down1, g_own = tie(up1, down1, g_own)
    low, high = along_y(g_own, 1), along_y(g_own, -1)
    up2, down2 = along_z(up1, 1), along_z(down1, -1)
    up3, down3 = along_z(up2, 1), along_z(down2, -1)
    g_far = along_y(low[:, :cut], 1), along_y(high[:, cut:], -1)
    far = along_z(up3[:, :cut], 1), along_z(down3[:, cut:], -1)
    far, g_far = tie(far, g_far)
    return ([own, down1, up1, down2, up2, down3, up3], far), ([g_own, high, low], g_far)


def scatter_both(out_terms, in_terms):
    own, p1, m1, p2, m2, p3, m3, far = out_terms
    g_own, g_p1, g_m1, g_far = in_terms
    half = own.shape[1] // 2
    up, down = along_z(far[:, :half], 1), along_z(far[:, half:], -1)
    g_up, g_down = along_y(g_far[:, :half], 1), along_y(g_far[:, half:], -1)
    up = jnp.concatenate([add(up, p3[:, :half]), p3[:, half:]], axis=1)
    down = jnp.concatenate([m3[:, :half], add(down, m3[:, half:])], axis=1)
    up, down = along_z(up, 1), along_z(down, -1)
    g_up = jnp.concatenate([add(g_up, g_p1[:, :half]), g_p1[:, half:]], axis=1)
    g_down = jnp.concatenate([g_m1[:, :half], add(g_down, g_m1[:, half:])], axis=1)
    g_up, g_down = along_y(g_up, 1), along_y(g_down, -1)
    up, down = along_z(add(up, p2), 1), along_z(add(down, m2), -1)
    up, down, g_up, g_down = tie(up, down, g_up, g_down)
    up, down = along_z(add(up, p1), 1), along_z(add(down, m1), -1)
    g_own, g_p1, g_m1, g_p2, g_m2, g_p3, g_m3, g_far = sum_split(N_Z, g_own, g_up, g_down)
    g_up, g_down = along_z(g_far, 1), along_z(g_m3, -1)
    g_up, g_down = along_z(add(g_up, g_p3), 1), along_z(add(g_down, g_m2), -1)
    up, down, g_up, g_down = tie(up, down, g_up, g_down)
    own, p1, m1, far = sum_split(N_Y, own, up, down)
    moved = along_y(p1, 1), along_y(m1, -1), along_y(far, 2)
    g_up, g_down = along_z(add(g_up, g_p2), 1), along_z(add(g_down, g_m1), -1)
    g_up = along_z(add(g_up, g_p1), 1)
    return (
        sum([m.astype(f32) for m in moved], own.astype(f32)).astype(bf16),
        (g_own.astype(f32) + g_up.astype(f32) + g_down.astype(f32)).astype(bf16),
    )


def turn_matrix(rows, first, second):
    source = np.arange(rows).reshape(first, second, -1).transpose(1, 0, 2).reshape(-1)
    return jnp.asarray(np.eye(rows, dtype=np.float32)[source], bf16)


def params(mib):
    return pltpu.CompilerParams(vmem_limit_bytes=mib * 2**20)


def cost(flops, moved):
    return pl.CostEstimate(flops=int(flops), bytes_accessed=int(moved), transcendentals=0)


WHOLE = pl.BlockSpec(memory_space=pltpu.VMEM)
LONG = pl.BlockSpec(memory_space=pltpu.HBM)
SCALAR = pl.BlockSpec(memory_space=pltpu.SMEM)


def in_hbm(value):
    return pltpu.with_memory_space_constraint(value, pltpu.HBM)


def columns_at(step, chunk):
    return pl.ds(pl.multiple_of(step * chunk, chunk), chunk)


def gather_matmul(blocks, far, weight, core, turn):
    n_blocks = len(blocks)
    size, width = blocks[0].shape
    rows = size * (n_blocks + 1)
    hidden = weight.shape[0]
    chunk = width // CHUNKS
    cut = far[0].shape[1]
    half = rows // 2

    def kernel(*refs):
        core_ref, *refs = refs
        block_refs, refs = refs[:n_blocks], refs[n_blocks:]
        (low, high, weight_ref), refs = refs[:3], refs[3:]
        if turn is not None:
            turn_ref, *refs = refs
        all_ref, keep_ref, give_ref, total, held, row_sems, weight_sems = refs
        at = n_blocks * size
        copies = []
        for side, (cols, last) in enumerate([(slice(0, cut), low), (slice(cut, width), high)]):
            moves = [
                (ref.at[:, cols], all_ref.at[i * size : (i + 1) * size, cols])
                for i, ref in enumerate(block_refs)
            ]
            moves.append((last, all_ref.at[at:, cols]))
            copies.append(
                [pltpu.make_async_copy(*m, row_sems.at[side, i]) for i, m in enumerate(moves)]
            )
        loads = [
            pltpu.make_async_copy(
                weight_ref.at[:, i * chunk : (i + 1) * chunk], held.at[i], weight_sems.at[i]
            )
            for i in range(CHUNKS)
        ]
        first = cut // chunk
        for c in copies[0] + loads[:first] + copies[1] + loads[first:]:
            c.start()
        for c in copies[0]:
            c.wait()

        def column(step):
            pltpu.make_async_copy(
                weight_ref.at[:, columns_at(step, chunk)], held.at[step], weight_sems.at[step]
            ).wait()
            return lax.dot_general(
                all_ref[:, columns_at(step, chunk)],
                held[step],
                (((1,), (1,)), ((), ())),
                preferred_element_type=f32,
            )

        total[...] = column(0)

        @pl.loop(1, first)
        def _(step):
            total[...] += column(step)

        for c in copies[1]:
            c.wait()

        @pl.loop(first, CHUNKS)
        def _(step):
            total[...] += column(step)

        if turn is not None:
            total[...] = jnp.dot(
                turn_ref[...], total[...].astype(bf16), preferred_element_type=f32
            )
        mine = core_ref[0]
        keep_ref[...] = total[pl.ds(pl.multiple_of(mine * half, half), half), :]
        give_ref[...] = total[pl.ds(pl.multiple_of((1 - mine) * half, half), half), :].astype(bf16)

    extra = [] if turn is None else [turn]
    return pl.pallas_call(
        kernel,
        in_specs=[SCALAR] + [LONG] * (n_blocks + 3) + [WHOLE] * len(extra),
        out_specs=[WHOLE] * 3,
        out_shape=[
            jax.ShapeDtypeStruct((rows, width), bf16),
            jax.ShapeDtypeStruct((half, hidden), f32),
            jax.ShapeDtypeStruct((half, hidden), bf16),
        ],
        scratch_shapes=[
            pltpu.VMEM((rows, hidden), f32),
            pltpu.VMEM((CHUNKS, hidden, chunk), bf16),
            pltpu.SemaphoreType.DMA((2, n_blocks + 1)),
            pltpu.SemaphoreType.DMA((CHUNKS,)),
        ],
        compiler_params=params(LIMIT),
        cost_estimate=cost(2 * rows * width * hidden, 2 * (2 * rows * width + width * hidden)),
    )(core, *map(in_hbm, blocks), *map(in_hbm, far), in_hbm(weight), *extra)


def matmul_scatter(own, other, weight, core, turn, turn_terms, n_blocks):
    half, hidden = own.shape
    rows = 2 * half
    width = weight.shape[1]
    chunk = width // CHUNKS
    size = rows // n_blocks

    def kernel(*refs):
        core_ref, own_ref, other_ref, weight_ref, turn_ref, full_ref, turned_ref, *refs = refs
        outs, (held, weight_sems) = refs[:n_blocks], refs[n_blocks:]
        for i in range(CHUNKS):
            pltpu.make_async_copy(
                weight_ref.at[:, i * chunk : (i + 1) * chunk], held.at[i], weight_sems.at[i]
            ).start()
        mine = core_ref[0]
        full_ref[pl.ds(pl.multiple_of(mine * half, half), half), :] = own_ref[...]
        full_ref[pl.ds(pl.multiple_of((1 - mine) * half, half), half), :] = other_ref[...]
        turned_ref[...] = jnp.dot(
            turn_ref[...], full_ref[...], preferred_element_type=f32
        ).astype(bf16)
        left = turned_ref if turn_terms else full_ref

        @pl.loop(0, CHUNKS)
        def _(step):
            here = columns_at(step, chunk)
            pltpu.make_async_copy(
                weight_ref.at[:, here], held.at[step], weight_sems.at[step]
            ).wait()
            term = jnp.dot(left[...], held[step], preferred_element_type=f32).astype(bf16)
            for i, out in enumerate(outs):
                out[:, here] = term[i * size : (i + 1) * size]

    return pl.pallas_call(
        kernel,
        in_specs=[SCALAR, WHOLE, WHOLE, LONG, WHOLE],
        out_specs=[WHOLE] * (2 + n_blocks),
        out_shape=[jax.ShapeDtypeStruct((rows, hidden), bf16)] * 2
        + [jax.ShapeDtypeStruct((size, width), bf16)] * n_blocks,
        scratch_shapes=[
            pltpu.VMEM((CHUNKS, hidden, chunk), bf16),
            pltpu.SemaphoreType.DMA((CHUNKS,)),
        ],
        compiler_params=params(LIMIT),
        cost_estimate=cost(2 * rows * width * hidden, 2 * (rows * width + width * hidden)),
    )(core, own, other, in_hbm(weight), turn)


def join(*blocks):
    width = blocks[0].shape[1]
    rows = sum(b.shape[0] for b in blocks)
    chunk = width // CHUNKS

    def kernel(*refs):
        *ins, out = refs

        @pl.loop(0, CHUNKS)
        def _(step):
            here = columns_at(step, chunk)
            out[:, here] = jnp.concatenate([r[:, here].astype(f32) for r in ins], axis=0).astype(bf16)

    return pl.pallas_call(
        kernel,
        in_specs=[WHOLE] * len(blocks),
        out_specs=WHOLE,
        out_shape=jax.ShapeDtypeStruct((rows, width), bf16),
        compiler_params=params(8),
        cost_estimate=cost(rows * width, 4 * rows * width),
    )(*blocks)


def sum_split(n_blocks, *terms):
    rows, width = terms[0].shape
    chunk = width // CHUNKS
    size = rows // n_blocks

    def kernel(*refs):
        ins, outs = refs[: len(terms)], refs[len(terms) :]

        @pl.loop(0, CHUNKS)
        def _(step):
            here = columns_at(step, chunk)
            total = ins[0][:, here].astype(f32)
            for r in ins[1:]:
                total += r[:, here].astype(f32)
            for i, out in enumerate(outs):
                out[:, here] = total[i * size : (i + 1) * size].astype(bf16)

    return pl.pallas_call(
        kernel,
        in_specs=[WHOLE] * len(terms),
        out_specs=[WHOLE] * n_blocks,
        out_shape=[jax.ShapeDtypeStruct((size, width), bf16)] * n_blocks,
        compiler_params=params(8),
        cost_estimate=cost(rows * width, 2 * (len(terms) + 1) * rows * width),
    )(*terms)


def half_sum(keep, give):
    chip = (keep + swap_core(give).astype(f32)).astype(bf16)
    return chip.astype(f32) + swap_x_hi(chip).astype(f32)


def column_sums(blocks):
    def ring_z(rows):
        r = [rows[20 * i : 20 * (i + 1)].astype(f32) for i in range(N_Z)]
        zero, p1, m1, p2, m2, p3, m3, far = r
        return ((zero + far) + (p2 + m2)) + ((p1 + m3) + (m1 + p3))

    own, p1, m1, far = [ring_z(blocks[160 * i : 160 * (i + 1)]) for i in range(N_Y)]
    total = (own + far) + (p1 + m1)
    total = total[:10] + total[10:]
    return jnp.sum(total, axis=0)


def shards(tokens, first_weight, first_bias, second_weight, second_bias, out_grad):
    core = lax.axis_index("gz").astype(jnp.int32).reshape(1) % 2
    rows = 640
    to_y, to_z = turn_matrix(rows, N_Z, N_Y), turn_matrix(rows, N_Y, N_Z)
    other = swap_x_lo(rows_of(tokens, out_grad))
    tokens_x, grad_x = rows_of(tokens, other[:10]), rows_of(out_grad, other[10:])

    token_parts, grad_parts = gather_both(tokens_x, grad_x)
    weight_in = first_weight.T
    token_rows, keep, give = gather_matmul(*token_parts, weight_in, core, to_y)
    chip = (keep + swap_core(give).astype(f32)).astype(bf16)
    grad_blocks, grad_far = grad_parts
    chip, *grad_blocks = tie(chip, *grad_blocks)
    pre_act = chip.astype(f32) + swap_x_hi(chip).astype(f32) + first_bias.astype(f32)
    grad_rows, keep, give = gather_matmul(grad_blocks, grad_far, second_weight, core, None)
    gelu_val, derivative = gelu_parts(pre_act)
    hidden_half = gelu_val.astype(bf16)
    hidden, _, *out_terms = matmul_scatter(
        hidden_half, swap_core(hidden_half), second_weight, core, to_z, True, N_Z
    )
    grad_half = (half_sum(keep, give) * derivative).astype(bf16)
    grad_pre, grad_pre_z, *in_terms = matmul_scatter(
        grad_half, swap_core(grad_half), weight_in, core, to_z, False, N_Y
    )

    out_rows, in_rows = scatter_both(out_terms, in_terms)
    output = (
        out_rows[:10].astype(f32) + swap_x_lo(out_rows[10:]).astype(f32) + second_bias.astype(f32)
    ).astype(bf16)
    tokens_grad = add(in_rows[:10], swap_x_lo(in_rows[10:]))

    first_grad = contract_rows(grad_pre_z, token_rows).astype(bf16).T
    bias_grad = jnp.sum(grad_pre.astype(f32), axis=0, keepdims=True).astype(bf16)
    second_grad = contract_rows(hidden, grad_rows).astype(bf16)
    return (
        output,
        tokens_grad,
        first_grad,
        bias_grad,
        second_grad,
        column_sums(grad_rows).astype(bf16),
    )


def solution(mesh):
    placed = (
        P(("gx", "gy"), "gz"),
        P("gz", ("gx", "gy")),
        P(None, ("gx", "gy")),
        P(("gx", "gy"), "gz"),
        P("gz"),
        P(("gx", "gy"), "gz"),
    )
    return jax.shard_map(
        shards,
        mesh=mesh,
        in_specs=placed,
        out_specs=(
            P(("gx", "gy"), "gz"),
            P(("gx", "gy"), "gz"),
            P("gz", ("gx", "gy")),
            P(None, ("gx", "gy")),
            P(("gx", "gy"), "gz"),
            P("gz"),
        ),
        check_vma=False,
    )
```

```python
import jax
import jax.numpy as jnp
import numpy as np
from jax import lax
from jax.experimental import pallas as pl
from jax.experimental.pallas import tpu as pltpu
from jax.sharding import PartitionSpec as P

N_Y, N_Z = 4, 8
CHUNKS = 7
LIMIT = 16
gelu_scale = 0.7978845608028654
gelu_cubic = 0.044715
f32, bf16 = jnp.float32, jnp.bfloat16


def gelu_parts(pre_act):
    inner = gelu_scale * (pre_act + gelu_cubic * pre_act * pre_act * pre_act)
    tangent = jnp.tanh(inner)
    gelu_val = 0.5 * pre_act * (1.0 + tangent)
    derivative = 0.5 * (1.0 + tangent) + 0.5 * pre_act * (1.0 - tangent * tangent) * gelu_scale * (
        1.0 + 3.0 * gelu_cubic * pre_act * pre_act
    )
    return (gelu_val, derivative)


def contract_rows(left, right):
    return lax.dot_general(left, right, (((0,), (0,)), ((), ())), preferred_element_type=f32)


def contract_cols(left, right):
    return lax.dot_general(left, right, (((1,), (1,)), ((), ())), preferred_element_type=f32)


def along_y(value, hops):
    pairs = [
        (y * N_Z + z, (y + hops) % N_Y * N_Z + z) for y in range(N_Y) for z in range(N_Z)
    ]
    return lax.ppermute(value, "gx", pairs)


def along_z(value, hops):
    pairs = [
        (y * N_Z + z, y * N_Z + (z + hops) % N_Z) for y in range(N_Y) for z in range(N_Z)
    ]
    return lax.ppermute(value, "gx", pairs)


def swap_x_lo(value):
    return lax.ppermute(value, "gy", [(0, 1), (1, 0)])


def swap_x_hi(value):
    return lax.ppermute(value, "gz", [(i, i ^ 2) for i in range(4)])


def swap_core(value):
    return lax.ppermute(value, "gz", [(i, i ^ 1) for i in range(4)])


def rows_of(*blocks):
    return jnp.concatenate(blocks, axis=0)


def tie(*values):
    return lax.optimization_barrier(values)


def add(left, right):
    return (left.astype(f32) + right.astype(f32)).astype(bf16)


def gather_both(tokens_x, grad_x):
    g_up1, g_down1 = along_z(grad_x, 1), along_z(grad_x, -1)
    small = [along_y(tokens_x, -1), along_y(tokens_x, 1), along_y(tokens_x, 2)]
    g_up2, g_down2 = along_z(g_up1, 1), along_z(g_down1, -1)
    own = join(tokens_x, *small)
    cut = own.shape[1] // CHUNKS * (CHUNKS // 2)
    g_up3, g_down3 = along_z(g_up2, 1), along_z(g_down2, -1)
    own, g_up3, g_down3 = tie(own, g_up3, g_down3)
    up1, down1 = along_z(own, 1), along_z(own, -1)
    g_own = join(grad_x, g_down1, g_up1, g_down2, g_up2, g_down3, g_up3, along_z(g_up3, 1))
    up1, down1, g_own = tie(up1, down1, g_own)
    low, high = along_y(g_own, 1), along_y(g_own, -1)
    up2, down2 = along_z(up1, 1), along_z(down1, -1)
    up3, down3 = along_z(up2, 1), along_z(down2, -1)
    g_far = along_y(low[:, :cut], 1), along_y(high[:, cut:], -1)
    far = along_z(up3[:, :cut], 1), along_z(down3[:, cut:], -1)
    far, g_far = tie(far, g_far)
    return ([own, down1, up1, down2, up2, down3, up3], far), ([g_own, high, low], g_far)


def scatter_both(out_terms, in_terms):
    own, p1, m1, p2, m2, p3, m3, far = out_terms
    g_own, g_p1, g_m1, g_far = in_terms
    half = own.shape[1] // 2
    up, down = along_z(far[:, :half], 1), along_z(far[:, half:], -1)
    g_up, g_down = along_y(g_far[:, :half], 1), along_y(g_far[:, half:], -1)
    up = jnp.concatenate([add(up, p3[:, :half]), p3[:, half:]], axis=1)
    down = jnp.concatenate([m3[:, :half], add(down, m3[:, half:])], axis=1)
    up, down = along_z(up, 1), along_z(down, -1)
    g_up = jnp.concatenate([add(g_up, g_p1[:, :half]), g_p1[:, half:]], axis=1)
    g_down = jnp.concatenate([g_m1[:, :half], add(g_down, g_m1[:, half:])], axis=1)
    g_up, g_down = along_y(g_up, 1), along_y(g_down, -1)
    up, down = along_z(add(up, p2), 1), along_z(add(down, m2), -1)
    up, down, g_up, g_down = tie(up, down, g_up, g_down)
    up, down = along_z(add(up, p1), 1), along_z(add(down, m1), -1)
    g_own, g_p1, g_m1, g_p2, g_m2, g_p3, g_m3, g_far = sum_split(N_Z, g_own, g_up, g_down)
    g_up, g_down = along_z(g_far, 1), along_z(g_m3, -1)
    g_up, g_down = along_z(add(g_up, g_p3), 1), along_z(add(g_down, g_m2), -1)
    up, down, g_up, g_down = tie(up, down, g_up, g_down)
    own, p1, m1, far = sum_split(N_Y, own, up, down)
    moved = along_y(p1, 1), along_y(m1, -1), along_y(far, 2)
    g_up, g_down = along_z(add(g_up, g_p2), 1), along_z(add(g_down, g_m1), -1)
    g_up = along_z(add(g_up, g_p1), 1)
    return (
        sum([m.astype(f32) for m in moved], own.astype(f32)).astype(bf16),
        (g_own.astype(f32) + g_up.astype(f32) + g_down.astype(f32)).astype(bf16),
    )


def turn_matrix(rows, first, second):
    source = np.arange(rows).reshape(first, second, -1).transpose(1, 0, 2).reshape(-1)
    return jnp.asarray(np.eye(rows, dtype=np.float32)[source], bf16)


def params(mib):
    return pltpu.CompilerParams(vmem_limit_bytes=mib * 2**20)


def cost(flops, moved):
    return pl.CostEstimate(flops=int(flops), bytes_accessed=int(moved), transcendentals=0)


WHOLE = pl.BlockSpec(memory_space=pltpu.VMEM)
LONG = pl.BlockSpec(memory_space=pltpu.HBM)
SCALAR = pl.BlockSpec(memory_space=pltpu.SMEM)


def in_hbm(value):
    return pltpu.with_memory_space_constraint(value, pltpu.HBM)


def columns_at(step, chunk):
    return pl.ds(pl.multiple_of(step * chunk, chunk), chunk)


def gather_matmul(blocks, far, weight, core, turn):
    n_blocks = len(blocks)
    size, width = blocks[0].shape
    rows = size * (n_blocks + 1)
    hidden = weight.shape[0]
    cut = far[0].shape[1]
    half = rows // 2

    def kernel(*refs):
        core_ref, *refs = refs
        block_refs, refs = refs[:n_blocks], refs[n_blocks:]
        (low, high, weight_ref), refs = refs[:3], refs[3:]
        if turn is not None:
            turn_ref, *refs = refs
        all_ref, keep_ref, give_ref, total, held, row_sems, weight_sems = refs
        at = n_blocks * size
        copies = []
        for side, (cols, last) in enumerate([(slice(0, cut), low), (slice(cut, width), high)]):
            moves = [
                (ref.at[:, cols], all_ref.at[i * size : (i + 1) * size, cols])
                for i, ref in enumerate(block_refs)
            ]
            moves.append((last, all_ref.at[at:, cols]))
            copies.append(
                [pltpu.make_async_copy(*m, row_sems.at[side, i]) for i, m in enumerate(moves)]
            )
        loads = [
            pltpu.make_async_copy(weight_ref.at[:, cols], held.at[:, cols], weight_sems.at[i])
            for i, cols in enumerate([slice(0, cut), slice(cut, width)])
        ]
        for i in range(2):
            for c in copies[i]:
                c.start()
            loads[i].start()

        def columns(i, cols):
            for c in copies[i]:
                c.wait()
            loads[i].wait()
            return lax.dot_general(
                all_ref[:, cols],
                held[:, cols],
                (((1,), (1,)), ((), ())),
                preferred_element_type=f32,
            )

        total[...] = columns(0, slice(0, cut))
        total[...] += columns(1, slice(cut, width))
        if turn is not None:
            total[...] = jnp.dot(
                turn_ref[...], total[...].astype(bf16), preferred_element_type=f32
            )
        mine = core_ref[0]
        keep_ref[...] = total[pl.ds(pl.multiple_of(mine * half, half), half), :]
        give_ref[...] = total[pl.ds(pl.multiple_of((1 - mine) * half, half), half), :].astype(bf16)

    extra = [] if turn is None else [turn]
    return pl.pallas_call(
        kernel,
        in_specs=[SCALAR] + [LONG] * (n_blocks + 3) + [WHOLE] * len(extra),
        out_specs=[WHOLE] * 3,
        out_shape=[
            jax.ShapeDtypeStruct((rows, width), bf16),
            jax.ShapeDtypeStruct((half, hidden), f32),
            jax.ShapeDtypeStruct((half, hidden), bf16),
        ],
        scratch_shapes=[
            pltpu.VMEM((rows, hidden), f32),
            pltpu.VMEM((hidden, width), bf16),
            pltpu.SemaphoreType.DMA((2, n_blocks + 1)),
            pltpu.SemaphoreType.DMA((2,)),
        ],
        compiler_params=params(LIMIT),
        cost_estimate=cost(2 * rows * width * hidden, 2 * (2 * rows * width + width * hidden)),
    )(core, *map(in_hbm, blocks), *map(in_hbm, far), in_hbm(weight), *extra)


def matmul_scatter(own, other, weight, core, turn, turn_terms, n_blocks):
    half, hidden = own.shape
    rows = 2 * half
    width = weight.shape[1]
    chunk = width // CHUNKS
    size = rows // n_blocks

    def kernel(*refs):
        core_ref, own_ref, other_ref, weight_ref, turn_ref, full_ref, turned_ref, *refs = refs
        outs, (held, weight_sems) = refs[:n_blocks], refs[n_blocks:]
        for i in range(CHUNKS):
            pltpu.make_async_copy(
                weight_ref.at[:, i * chunk : (i + 1) * chunk], held.at[i], weight_sems.at[i]
            ).start()
        mine = core_ref[0]
        full_ref[pl.ds(pl.multiple_of(mine * half, half), half), :] = own_ref[...]
        full_ref[pl.ds(pl.multiple_of((1 - mine) * half, half), half), :] = other_ref[...]
        turned_ref[...] = jnp.dot(
            turn_ref[...], full_ref[...], preferred_element_type=f32
        ).astype(bf16)
        left = turned_ref if turn_terms else full_ref

        @pl.loop(0, CHUNKS)
        def _(step):
            here = columns_at(step, chunk)
            pltpu.make_async_copy(
                weight_ref.at[:, here], held.at[step], weight_sems.at[step]
            ).wait()
            term = jnp.dot(left[...], held[step], preferred_element_type=f32).astype(bf16)
            for i, out in enumerate(outs):
                out[:, here] = term[i * size : (i + 1) * size]

    return pl.pallas_call(
        kernel,
        in_specs=[SCALAR, WHOLE, WHOLE, LONG, WHOLE],
        out_specs=[WHOLE] * (2 + n_blocks),
        out_shape=[jax.ShapeDtypeStruct((rows, hidden), bf16)] * 2
        + [jax.ShapeDtypeStruct((size, width), bf16)] * n_blocks,
        scratch_shapes=[
            pltpu.VMEM((CHUNKS, hidden, chunk), bf16),
            pltpu.SemaphoreType.DMA((CHUNKS,)),
        ],
        compiler_params=params(LIMIT),
        cost_estimate=cost(2 * rows * width * hidden, 2 * (rows * width + width * hidden)),
    )(core, own, other, in_hbm(weight), turn)


def join(*blocks):
    width = blocks[0].shape[1]
    rows = sum(b.shape[0] for b in blocks)
    chunk = width // CHUNKS

    def kernel(*refs):
        *ins, out = refs

        @pl.loop(0, CHUNKS)
        def _(step):
            here = columns_at(step, chunk)
            out[:, here] = jnp.concatenate([r[:, here].astype(f32) for r in ins], axis=0).astype(bf16)

    return pl.pallas_call(
        kernel,
        in_specs=[WHOLE] * len(blocks),
        out_specs=WHOLE,
        out_shape=jax.ShapeDtypeStruct((rows, width), bf16),
        compiler_params=params(8),
        cost_estimate=cost(rows * width, 4 * rows * width),
    )(*blocks)


def sum_split(n_blocks, *terms):
    rows, width = terms[0].shape
    chunk = width // CHUNKS
    size = rows // n_blocks

    def kernel(*refs):
        ins, outs = refs[: len(terms)], refs[len(terms) :]

        @pl.loop(0, CHUNKS)
        def _(step):
            here = columns_at(step, chunk)
            total = ins[0][:, here].astype(f32)
            for r in ins[1:]:
                total += r[:, here].astype(f32)
            for i, out in enumerate(outs):
                out[:, here] = total[i * size : (i + 1) * size].astype(bf16)

    return pl.pallas_call(
        kernel,
        in_specs=[WHOLE] * len(terms),
        out_specs=[WHOLE] * n_blocks,
        out_shape=[jax.ShapeDtypeStruct((size, width), bf16)] * n_blocks,
        compiler_params=params(8),
        cost_estimate=cost(rows * width, 2 * (len(terms) + 1) * rows * width),
    )(*terms)


def half_sum(keep, give):
    chip = (keep + swap_core(give).astype(f32)).astype(bf16)
    return chip.astype(f32) + swap_x_hi(chip).astype(f32)


def column_sums(blocks):
    def ring_z(rows):
        r = [rows[20 * i : 20 * (i + 1)].astype(f32) for i in range(N_Z)]
        zero, p1, m1, p2, m2, p3, m3, far = r
        return ((zero + far) + (p2 + m2)) + ((p1 + m3) + (m1 + p3))

    own, p1, m1, far = [ring_z(blocks[160 * i : 160 * (i + 1)]) for i in range(N_Y)]
    total = (own + far) + (p1 + m1)
    total = total[:10] + total[10:]
    return jnp.sum(total, axis=0)


def shards(tokens, first_weight, first_bias, second_weight, second_bias, out_grad):
    core = lax.axis_index("gz").astype(jnp.int32).reshape(1) % 2
    rows = 640
    to_y, to_z = turn_matrix(rows, N_Z, N_Y), turn_matrix(rows, N_Y, N_Z)
    other = swap_x_lo(rows_of(tokens, out_grad))
    tokens_x, grad_x = rows_of(tokens, other[:10]), rows_of(out_grad, other[10:])

    token_parts, grad_parts = gather_both(tokens_x, grad_x)
    weight_in = first_weight.T
    token_rows, keep, give = gather_matmul(*token_parts, weight_in, core, to_y)
    chip = (keep + swap_core(give).astype(f32)).astype(bf16)
    grad_blocks, grad_far = grad_parts
    chip, *grad_blocks = tie(chip, *grad_blocks)
    pre_act = chip.astype(f32) + swap_x_hi(chip).astype(f32) + first_bias.astype(f32)
    grad_rows, keep, give = gather_matmul(grad_blocks, grad_far, second_weight, core, None)
    gelu_val, derivative = gelu_parts(pre_act)
    hidden_half = gelu_val.astype(bf16)
    hidden, _, *out_terms = matmul_scatter(
        hidden_half, swap_core(hidden_half), second_weight, core, to_z, True, N_Z
    )
    grad_half = (half_sum(keep, give) * derivative).astype(bf16)
    grad_pre, grad_pre_z, *in_terms = matmul_scatter(
        grad_half, swap_core(grad_half), weight_in, core, to_z, False, N_Y
    )

    out_rows, in_rows = scatter_both(out_terms, in_terms)
    output = (
        out_rows[:10].astype(f32) + swap_x_lo(out_rows[10:]).astype(f32) + second_bias.astype(f32)
    ).astype(bf16)
    tokens_grad = add(in_rows[:10], swap_x_lo(in_rows[10:]))

    first_grad = contract_rows(grad_pre_z, token_rows).astype(bf16).T
    bias_grad = jnp.sum(grad_pre.astype(f32), axis=0, keepdims=True).astype(bf16)
    second_grad = contract_rows(hidden, grad_rows).astype(bf16)
    return (
        output,
        tokens_grad,
        first_grad,
        bias_grad,
        second_grad,
        column_sums(grad_rows).astype(bf16),
    )


def solution(mesh):
    placed = (
        P(("gx", "gy"), "gz"),
        P("gz", ("gx", "gy")),
        P(None, ("gx", "gy")),
        P(("gx", "gy"), "gz"),
        P("gz"),
        P(("gx", "gy"), "gz"),
    )
    return jax.shard_map(
        shards,
        mesh=mesh,
        in_specs=placed,
        out_specs=(
            P(("gx", "gy"), "gz"),
            P(("gx", "gy"), "gz"),
            P("gz", ("gx", "gy")),
            P(None, ("gx", "gy")),
            P(("gx", "gy"), "gz"),
            P("gz"),
        ),
        check_vma=False,
    )
```
